512 devices in a mesh: ka: 64 (over z, x_hi, core), ga: 8 (over y, x_lo).
Axes of the slice: x: 4 (x_hi: 2, x_lo: 2; x = x_hi * 2 + x_lo), y: 4, z: 16, core: 2. Of those that a mesh axis runs over, the one named last changes fastest.
Arguments:
- orbitals: bfloat16 [128, 4096, 256], P('ka', 'ga'), may hold values from -1.5 to 1.5
- minus_table: int32 [2, 128], replicated, may hold values from 0 to 127, as said below
- points: int32 [512], replicated, may hold values from 0 to 4095, as said below
Outputs:
- pair_matrix: float32 [512, 2, 2, 4096], P('ka', None, None, 'ga')
The draws below stay inside these ranges and needn't reach their ends.
Inputs may be any that keep to these rules, and one draw needn't show every extreme that they name: `minus_table`: row q holds (k - s) mod 128 for every k, with one shift s for the row that is a nonzero multiple of 2; the two rows have different shifts. `points`: distinct grid indices; 0 and 4095 are among them.
All inputs are finite; a program needn't handle non-finite values.
Results may differ from the reference program's by a relative error of at most 0.0012.
Values may be sent and summed in bfloat16 or wider, within the bound.
A program may use at most 64 MiB of HBM per device.

```python
import math
import jax
import jax.numpy as jnp
from jax import lax

NB = 128
NPTS = 512
K_DEV = 2
NK = 128
NGRID = 4096
N_KA = 64


def draw_minus_table(key, part):
    key = jax.random.fold_in(key, 12)
    first_key, second_key = jax.random.split(key)
    first_shift = jax.random.randint(first_key, (), 1, N_KA)
    offset = jax.random.randint(second_key, (), 1, N_KA - 1)
    second_shift = 1 + (first_shift - 1 + offset) % (N_KA - 1)
    shifts = jnp.stack([first_shift, second_shift]) * K_DEV
    kpoints = jnp.arange(NK, dtype=jnp.int32)
    return ((kpoints[None, :] - shifts[:, None]) % NK).astype(jnp.int32)


def draw_points(key, part):
    key = jax.random.fold_in(key, 11)
    inner = jax.random.permutation(key, NGRID - 2)[:NPTS - 2] + 1
    ends = jnp.array([0, NGRID - 1], dtype=jnp.int32)
    return jnp.concatenate([ends[:1], inner.astype(jnp.int32), ends[1:]]).astype(jnp.int32)


def level_of(rng, shape, cuts, least, largest):
    level, own = 1.0, jax.random.fold_in(rng, 6)
    for dim, parts in cuts:
        heights = jnp.exp(jax.random.uniform(jax.random.fold_in(own, dim), (parts,), jnp.float32, least / len(cuts), largest / len(cuts)))
        level = level * jnp.repeat(heights, shape[dim] // parts).reshape([-1 if axis == dim else 1 for axis in range(len(shape))])
    return level


def scatter_about(rng, shape, width, reach, cuts=(), held_as=jnp.bfloat16):
    entries = jax.random.normal(rng, shape, jnp.float32) * width
    if len(cuts) > 0:
        entries = level_of(rng, shape, cuts, -0.22, 0.18) * entries
    return jnp.clip(entries, min=-reach, max=reach).astype(held_as)


def setup_inputs(seed: int = 0) -> dict:
    splits = jax.random.split(jax.random.key(seed), 4)
    return {
        "orbitals": scatter_about(splits[0], (NK, NGRID, 2 * NB), ((2 * NB) ** -0.25), 1.5, ((0, 64), (1, 8))),
        "minus_table": draw_minus_table(jax.random.fold_in(splits[3], 71), 0),
        "points": draw_points(jax.random.fold_in(splits[3], 71), 0),
    }


def pair_field(field_rows, collected):
    halfway = collected.shape[1] // 2
    rotated = jnp.concatenate([-collected[:, halfway:], collected[:, :halfway]], axis=1)
    stacked = jnp.concatenate([collected, rotated], axis=0)
    product = lax.dot_general(stacked, field_rows, (((1,), (1,)), ((), ())), preferred_element_type=jnp.float32)
    rounded = lax.optimization_barrier(product.astype(jnp.bfloat16))
    return rounded.astype(jnp.float32)

def reference(orbitals, minus_table, points):
    npoints = points.shape[0]

    def advance(total, kpoint):
        own_field = pair_field(orbitals[kpoint], orbitals[kpoint][points])
        pieces = []
        for transfer in range(minus_table.shape[0]):
            other_k = minus_table[transfer, kpoint]
            other_rows = orbitals[other_k]
            other_field = pair_field(other_rows, other_rows[points])
            real_part = own_field[:npoints] * other_field[:npoints] + own_field[npoints:] * other_field[npoints:]
            imag_part = own_field[npoints:] * other_field[:npoints] - own_field[:npoints] * other_field[npoints:]
            pieces.append(jnp.stack([real_part, imag_part], axis=1))
        return (total + jnp.stack(pieces, axis=1), None)
    initial = jnp.zeros((npoints, minus_table.shape[0], 2, orbitals.shape[1]), jnp.float32)
    total, unused = lax.scan(advance, initial, jnp.arange(orbitals.shape[0], dtype=jnp.int32))
    return total * (1.0 / math.sqrt(NK))
```

```python
import math

import jax
import jax.numpy as jnp
from jax import lax
from jax.sharding import PartitionSpec as P


def on_device(orbitals, minus_table, points):
    kdevice, slab_size, channels = orbitals.shape
    cycle_size = lax.axis_size("ka")
    total_k = kdevice * cycle_size
    transfers = minus_table.shape[0]
    npts = points.shape[0]
    block = npts // cycle_size
    half = channels // 2
    local_rows = points - lax.axis_index("ga") * slab_size
    hot = (local_rows[:, None] == jnp.arange(slab_size)[None, :]).astype(jnp.bfloat16)
    picked = jnp.einsum("pg,kgc->kpc", hot, orbitals, preferred_element_type=jnp.float32)
    rows = lax.psum(picked.astype(jnp.bfloat16), "ga")
    rotated = jnp.concatenate([-rows[:, :, half:], rows[:, :, :half]], axis=2)
    parts = jnp.stack(
        [r.reshape(kdevice, cycle_size, block, channels) for r in (rows, rotated)], axis=2
    )
    stacked = parts.reshape(kdevice, cycle_size * 2 * block, channels)
    product = jnp.einsum("kpc,kgc->kpg", stacked, orbitals, preferred_element_type=jnp.float32)
    field = product.astype(jnp.bfloat16).reshape(kdevice, cycle_size, 2 * block, slab_size)
    arrived = lax.all_to_all(field.transpose(1, 0, 2, 3), "ka", 0, 0, tiled=True)
    own = arrived.reshape(total_k, 2, block, slab_size)
    twice = jnp.concatenate([own, own], axis=0)
    mine = own.astype(jnp.float32)
    pieces = []
    for transfer in range(transfers):
        other = lax.dynamic_slice_in_dim(twice, minus_table[transfer, 0], total_k, 0).astype(jnp.float32)
        real = jnp.sum(mine[:, 0] * other[:, 0] + mine[:, 1] * other[:, 1], axis=0)
        imag = jnp.sum(mine[:, 1] * other[:, 0] - mine[:, 0] * other[:, 1], axis=0)
        pieces.append(jnp.stack([real, imag], axis=1))
    return jnp.stack(pieces, axis=1) * (1.0 / math.sqrt(total_k))


def solution(mesh):
    placed = (P("ka", "ga", None), P(), P())
    return jax.shard_map(
        on_device, mesh=mesh, in_specs=placed, out_specs=P("ka", None, None, "ga"), check_vma=False
    )
```

```python
import functools
import math

import jax
import jax.numpy as jnp
from jax import lax
from jax.experimental import pallas as pl
from jax.experimental.pallas import tpu as pltpu
from jax.sharding import PartitionSpec as P

MESH = pl.DeviceIdType.MESH
F32 = jnp.float32
BF16 = jnp.bfloat16


def kernel(
    n_ka, n_ga, scale,
    table_ref, points_ref, orb_ref, out_ref,
    hot, masked, parts, rows, send, recv,
    rs_send, rs_recv, ag_send, ag_recv, x_send, x_recv, own_sem,
):
    kdev, slab, channels = orb_ref.shape
    half = channels // 2
    total_k = kdev * n_ka
    n_z = n_ka // 4
    me, g = lax.axis_index("ka"), lax.axis_index("ga")
    z = me // 4
    zrows = points_ref.shape[0] // n_z
    block = zrows // 4

    barrier = pltpu.get_barrier_semaphore()

    @pl.loop(1, n_ga)
    def _(i):
        pl.semaphore_signal(barrier, inc=1, device_id={"ga": (g + i) % n_ga}, device_id_type=MESH)

    @pl.loop(1, n_ka)
    def _(i):
        pl.semaphore_signal(barrier, inc=1, device_id={"ka": (me + i) % n_ka}, device_id_type=MESH)

    def z_of(b, jz):
        offset = (b + 1) if jz == 0 else (n_z - 1 - b) * (1 - b // (n_ga - 1))
        return (z + offset) % n_z

    grid_row = lax.broadcasted_iota(jnp.int32, (zrows, slab), 1) + g * slab
    for b in range(n_ga):
        for jz in range(2):
            index = points_ref[pl.ds(pl.multiple_of(z_of(b, jz) * zrows, zrows), zrows), :]
            hot[pl.ds((2 * b + jz) * zrows, zrows), :] = (index == grid_row).astype(F32).astype(BF16)
    for k in range(kdev):
        picked = jnp.dot(hot[...], orb_ref[k], preferred_element_type=F32).astype(BF16)
        masked[:, :, k * channels:(k + 1) * channels] = picked.reshape(n_ga, 2 * zrows, channels)

    pl.semaphore_wait(barrier, n_ga - 1 + n_ka - 1)

    @pl.loop(1, n_ga)
    def _(i):
        to = (g + n_ga - i) % n_ga
        pltpu.make_async_remote_copy(
            src_ref=masked.at[to], dst_ref=parts.at[g], send_sem=rs_send, recv_sem=rs_recv,
            device_id={"ga": to}, device_id_type=MESH).start()

    parts[g] = masked[g]
    arrivals = parts.at[pl.ds(0, n_ga - 1)]
    pltpu.make_async_copy(arrivals, arrivals, rs_recv).wait()
    summed = parts[0].astype(F32)
    for i in range(1, n_ga):
        summed = summed + parts[i].astype(F32)
    rows[g] = summed.astype(BF16)

    @pl.loop(1, n_ga)
    def _(i):
        pltpu.make_async_remote_copy(
            src_ref=rows.at[g], dst_ref=rows.at[g], send_sem=ag_send, recv_sem=ag_recv.at[g],
            device_id={"ga": (g + n_ga - i) % n_ga}, device_id_type=MESH).start()

    @pl.loop(0, n_ga)
    def _(i):
        b = (g + i) % n_ga

        @pl.when(i > 0)
        def _():
            pltpu.make_async_copy(rows.at[b], rows.at[b], ag_recv.at[b]).wait()

        for k in range(kdev):
            c = rows[b, :, k * channels:(k + 1) * channels].astype(F32)
            rotated = jnp.concatenate([-c[:, half:], c[:, :half]], axis=1)
            both = jnp.concatenate(
                [c.reshape(8, block, channels), rotated.reshape(8, block, channels)], axis=1)
            left = both.reshape(16 * block, channels).astype(BF16)
            field = lax.dot_general(
                left, orb_ref[k], (((1,), (1,)), ((), ())), preferred_element_type=F32)
            send[b, :, k] = field.astype(BF16).reshape(8, 2 * block, slab)

        for j in range(8):
            to = 4 * z_of(b, j // 4) + j % 4

            @pl.when(to != me)
            def _():
                pltpu.make_async_remote_copy(
                    src_ref=send.at[b, j], dst_ref=recv.at[pl.ds(kdev * me, kdev)],
                    send_sem=x_send, recv_sem=x_recv,
                    device_id={"ka": to}, device_id_type=MESH).start()

            @pl.when(to == me)
            def _():
                pltpu.make_async_copy(
                    send.at[b, j], recv.at[pl.ds(kdev * me, kdev)], own_sem).start()

    def drain(ref, sem):
        pltpu.make_async_copy(ref, ref, sem).wait()

    drain(send.at[0, 0], own_sem)
    drain(recv.at[pl.ds(0, total_k - kdev)], x_recv)

    shifts = [table_ref[q, 0] for q in range(2)]

    def step(k, totals):
        own = recv[k].astype(F32)
        own_re, own_im = own[:block], own[block:]
        new = []
        for q in range(2):
            other = recv[lax.rem(k + shifts[q], total_k)].astype(F32)
            re, im = other[:block], other[block:]
            new.append(totals[2 * q] + (own_re * re + own_im * im))
            new.append(totals[2 * q + 1] + (own_im * re - own_re * im))
        return tuple(new)

    zero = jnp.zeros((block, slab), F32)
    totals = lax.fori_loop(0, total_k, step, (zero,) * 4, unroll=4)
    for i in range(4):
        out_ref[i] = totals[i] * scale

    drain(masked.at[pl.ds(0, n_ga - 1)], rs_send)
    drain(rows.at[pl.ds(0, n_ga - 1)], ag_send)
    drain(recv.at[pl.ds(0, total_k - kdev)], x_send)


def on_device(orbitals, minus_table, points):
    kdev, slab, channels = orbitals.shape
    n_ka, n_ga = lax.axis_size("ka"), lax.axis_size("ga")
    npts = points.shape[0]
    block = npts // n_ka
    total_k = kdev * n_ka
    mine = npts // n_ga
    vmem = pl.BlockSpec(memory_space=pltpu.VMEM)
    dma = pltpu.SemaphoreType.DMA
    out = pl.pallas_call(
        functools.partial(kernel, n_ka, n_ga, 1.0 / math.sqrt(total_k)),
        out_shape=jax.ShapeDtypeStruct((4, block, slab), F32),
        in_specs=[pl.BlockSpec(memory_space=pltpu.SMEM), vmem, vmem],
        out_specs=vmem,
        scratch_shapes=[
            pltpu.VMEM((npts, slab), BF16),
            pltpu.VMEM((n_ga, mine, kdev * channels), BF16),
            pltpu.VMEM((n_ga, mine, kdev * channels), BF16),
            pltpu.VMEM((n_ga, mine, kdev * channels), BF16),
            pltpu.VMEM((n_ga, 8, kdev, 2 * block, slab), BF16),
            pltpu.VMEM((total_k, 2 * block, slab), BF16),
            dma, dma, dma, dma((n_ga,)), dma, dma, dma,
        ],
        compiler_params=pltpu.CompilerParams(
            collective_id=0, has_side_effects=True, vmem_limit_bytes=32 * 1024 * 1024),
    )(minus_table, points.reshape(npts, 1), orbitals)
    return out.reshape(2, 2, block, slab).transpose(2, 0, 1, 3)


def solution(mesh):
    placed = (P("ka", "ga", None), P(), P())
    return jax.shard_map(
        on_device, mesh=mesh, in_specs=placed, out_specs=P("ka", None, None, "ga"), check_vma=False
    )
```

```python
import functools
import math

import jax
import jax.numpy as jnp
from jax import lax
from jax.experimental import pallas as pl
from jax.experimental.pallas import tpu as pltpu
from jax.sharding import PartitionSpec as P

MESH = pl.DeviceIdType.MESH
F32 = jnp.float32
BF16 = jnp.bfloat16
NZ, NX, NY = 16, 4, 4
PLANE = NX * NY


def kernel(
    scale,
    table_ref, points_ref, orb_ref, out_ref,
    hot, masked, parts, rows, grid, fields, stage, tiles, got,
    rs_send, rs_recv, grid_send, grid_recv, gridx_send, rows_send, rows_recv, rowsy_send,
    pair_send, pair_recv, tile_send, tile_recv,
):
    kdev, slab, channels = orb_ref.shape
    half = channels // 2
    chunk = slab // NZ
    total_k = kdev * 4 * NZ
    me, g = lax.axis_index("ka"), lax.axis_index("ga")
    z, x_hi, core = me // 4, (me // 2) % 2, me % 2
    y, x_lo = g // 2, g % 2
    x = 2 * x_hi + x_lo
    place = x * NY + y
    in_turn = (1 - (z // 8 - x_lo) ** 2) * (1 - (core - x_lo) ** 2)

    def in_plane(xx, yy):
        return {"ka": 4 * z + 2 * (xx // 2) + core, "ga": 2 * yy + xx % 2}

    def send(src, dst, send_sem, recv_sem, to):
        pltpu.make_async_remote_copy(
            src_ref=src, dst_ref=dst, send_sem=send_sem, recv_sem=recv_sem,
            device_id=to, device_id_type=MESH).start()

    def drain(ref, sem):
        pltpu.make_async_copy(ref, ref, sem).wait()

    barrier = pltpu.get_barrier_semaphore()

    def greet(to):
        pl.semaphore_signal(barrier, inc=1, device_id=to, device_id_type=MESH)

    @pl.loop(1, NZ)
    def _(i):
        greet({"ka": (me + 4 * i) % (4 * NZ)})

    @pl.loop(1, PLANE)
    def _(i):
        to = (place + i) % PLANE
        greet(in_plane(to // NY, to % NY))

    greet({"ka": me + 1 - 2 * core})

    @pl.loop(0, NZ)
    def _(zz):
        @pl.when((in_turn == 0) | (zz != z))
        def _():
            greet({"ka": 4 * zz + 2 * x_hi + x_lo, "ga": 2 * y + z // 8})

    grid_row = lax.broadcasted_iota(jnp.int32, hot.shape, 0) + g * slab
    hot[...] = (points_ref[...] == grid_row).astype(F32).astype(BF16)
    for k in range(kdev):
        picked = lax.dot_general(
            hot[...], orb_ref[k], (((0,), (0,)), ((), ())), preferred_element_type=F32)
        masked[:, :, :, :, k * channels:(k + 1) * channels] = picked.astype(BF16).reshape(
            masked.shape[:4] + (channels,))

    pl.semaphore_wait(barrier, (NZ - 1) + (PLANE - 1) + 1 + NZ - in_turn)

    @pl.loop(1, PLANE)
    def _(i):
        to = (place + i) % PLANE
        xx, yy = to // NY, to % NY
        send(masked.at[4 * (xx % 2) + yy, :, xx // 2], parts.at[place],
             rs_send, rs_recv, in_plane(xx, yy))

    @pl.loop(1, NZ)
    def _(i):
        zz = (z + NZ + ((i + 1) // 2) * (2 * (i % 2) - 1)) % NZ
        send(orb_ref.at[:, pl.ds(pl.multiple_of(chunk * zz, chunk), chunk)], grid.at[x, z],
             grid_send, grid_recv.at[x, z], {"ka": 4 * zz + me % 4})

    def spread_grid(zz):
        @pl.loop(1, NX)
        def _(i):
            send(grid.at[x, zz], grid.at[x, zz], gridx_send, grid_recv.at[x, zz],
                 in_plane((x + i) % NX, y))

    def spread_rows(zz):
        @pl.loop(1, NY)
        def _(i):
            send(rows.at[y, zz], rows.at[y, zz], rowsy_send, rows_recv.at[y, zz],
                 in_plane(x, (y + i) % NY))

    def pass_rows(zz, to):
        send(rows.at[y, zz], rows.at[y, zz], rows_send, rows_recv.at[y, zz],
             {"ka": 4 * ((to + NZ) % NZ) + me % 4})

    grid[x, z] = orb_ref[:, pl.ds(pl.multiple_of(chunk * z, chunk), chunk), :]
    spread_grid(z)

    parts[place] = masked[4 * x_lo + y, :, x_hi]
    drain(parts.at[pl.ds(0, PLANE - 1)], rs_recv)
    for h in range(2):
        summed = parts[8 * h].astype(F32)
        for i in range(1, 8):
            summed = summed + parts[8 * h + i].astype(F32)
        rows[y, z, h] = summed.astype(BF16)
    pass_rows(z, z + 1)
    pass_rows(z, z - 1)
    spread_rows(z)

    @pl.loop(1, NZ // 2 + 1)
    def _(t):
        down = (z + NZ - t) % NZ
        drain(rows.at[y, down], rows_recv.at[y, down])

        @pl.when(t < NZ // 2)
        def _():
            pass_rows(down, z + 1)

        spread_rows(down)
        up = (z + t) % NZ

        @pl.when(t < NZ // 2)
        def _():
            drain(rows.at[y, up], rows_recv.at[y, up])

            @pl.when(t < NZ // 2 - 1)
            def _():
                pass_rows(up, z - 1)

            spread_rows(up)

        drain(grid.at[x, down], grid_recv.at[x, down])
        spread_grid(down)

        @pl.when(t < NZ // 2)
        def _():
            drain(grid.at[x, up], grid_recv.at[x, up])
            spread_grid(up)

    @pl.loop(0, NZ)
    def _(i):
        zz = (z + NZ + ((i + 1) // 2) * (2 * (i % 2) - 1)) % NZ

        @pl.loop(1, NX)
        def _(j):
            xx = (x + j) % NX
            drain(grid.at[xx, zz], grid_recv.at[xx, zz])

        @pl.loop(1, NY)
        def _(j):
            yy = (y + j) % NY
            drain(rows.at[yy, zz], rows_recv.at[yy, zz])

        for h in range(2):
            for k in range(kdev):
                picked = rows[:, zz, h, :, :, k * channels:(k + 1) * channels].reshape(
                    NY * 32, channels)
                stack = []
                for lo in (core, 1 - core):
                    phi = grid[2 * h + lo, zz, k]
                    stack += [phi, jnp.concatenate([phi[:, half:], -phi[:, :half]], axis=1)]
                field = lax.dot_general(
                    jnp.concatenate(stack, axis=0), picked, (((1,), (1,)), ((), ())),
                    preferred_element_type=F32).astype(BF16)
                fields[8 * zz + 4 * h + 2 * core + k] = field[:2 * chunk]
                stage[zz, h, k] = field[2 * chunk:]
            send(stage.at[zz, h], fields.at[pl.ds(8 * zz + 4 * h + 2 * core, kdev)],
                 pair_send, pair_recv, {"ka": me + 1 - 2 * core})

    drain(stage, pair_recv)

    shifts = [table_ref[q, 0] for q in range(2)]

    def step(k, totals):
        own = fields[k].astype(F32)
        own_re, own_im = own[:chunk], own[chunk:]
        new = []
        for q in range(2):
            other = fields[lax.rem(k + shifts[q], total_k)].astype(F32)
            re, im = other[:chunk], other[chunk:]
            new.append(totals[2 * q] + (own_re * re + own_im * im))
            new.append(totals[2 * q + 1] + (own_im * re - own_re * im))
        return tuple(new)

    zero = jnp.zeros((chunk, 128), F32)
    totals = lax.fori_loop(0, total_k, step, (zero,) * 4, unroll=4)
    tiles[...] = (jnp.concatenate(totals, axis=0) * scale).T.reshape(tiles.shape)

    @pl.loop(0, 16)
    def _(j):
        zz, cc = 8 * x_lo + j // 2, j % 2
        stays = (in_turn == 1) & (zz == z) & (cc == core)

        @pl.when(stays)
        def _():
            pltpu.make_async_copy(tiles.at[j], got.at[z], tile_recv).start()

        @pl.when(jnp.logical_not(stays))
        def _():
            send(tiles.at[j], got.at[z], tile_send, tile_recv,
                 {"ka": 4 * zz + 2 * x_hi + cc, "ga": 2 * y + core})

    drain(got, tile_recv)
    for i in range(4):
        out_ref[i] = jnp.concatenate(
            [got[zz, :, chunk * i:chunk * (i + 1)] for zz in range(NZ)], axis=1)

    drain(parts.at[pl.ds(0, PLANE - 1)], rs_send)
    drain(grid.at[0, pl.ds(0, NZ - 1)], grid_send)
    drain(grid.at[pl.ds(0, NX - 1)], gridx_send)
    drain(rows.at[0, pl.ds(0, NZ - 1)], rows_send)
    drain(rows.at[pl.ds(0, NY - 1)], rowsy_send)
    drain(stage, pair_send)

    @pl.when(in_turn == 1)
    def _():
        drain(tiles.at[pl.ds(0, 15)], tile_send)

    @pl.when(in_turn == 0)
    def _():
        drain(tiles, tile_send)


def on_device(orbitals, minus_table, points):
    kdev, slab, channels = orbitals.shape
    npts = points.shape[0]
    total_k = kdev * 4 * NZ
    chunk = slab // NZ
    wide = kdev * channels
    vmem = pl.BlockSpec(memory_space=pltpu.VMEM)
    dma = pltpu.SemaphoreType.DMA
    out = pl.pallas_call(
        functools.partial(kernel, 1.0 / math.sqrt(total_k)),
        out_shape=jax.ShapeDtypeStruct((4, 8, slab), F32),
        in_specs=[pl.BlockSpec(memory_space=pltpu.SMEM), vmem, vmem],
        out_specs=vmem,
        scratch_shapes=[
            pltpu.VMEM((slab, npts), BF16),
            pltpu.VMEM((8, 2, 2, 16, wide), BF16),
            pltpu.VMEM((PLANE, 2, 16, wide), BF16),
            pltpu.VMEM((NY, NZ, 2, 2, 16, wide), BF16),
            pltpu.VMEM((NX, NZ, kdev, chunk, channels), BF16),
            pltpu.VMEM((total_k, 2 * chunk, 128), BF16),
            pltpu.VMEM((NZ, 2, kdev, 2 * chunk, 128), BF16),
            pltpu.VMEM((16, 8, 128), F32),
            pltpu.VMEM((NZ, 8, 128), F32),
            dma, dma, dma, dma((NX, NZ)), dma, dma, dma((NY, NZ)), dma,
            dma, dma, dma, dma,
        ],
        compiler_params=pltpu.CompilerParams(
            collective_id=0, has_side_effects=True, vmem_limit_bytes=40 * 1024 * 1024),
    )(minus_table, points.reshape(1, npts), orbitals)
    return out.reshape(2, 2, 8, slab).transpose(2, 0, 1, 3)


def solution(mesh):
    placed = (P("ka", "ga", None), P(), P())
    return jax.shard_map(
        on_device, mesh=mesh, in_specs=placed, out_specs=P("ka", None, None, "ga"), check_vma=False
    )
```

```python
import functools
import math

import jax
import jax.numpy as jnp
from jax import lax
from jax.experimental import pallas as pl
from jax.experimental.pallas import tpu as pltpu
from jax.sharding import PartitionSpec as P

MESH = pl.DeviceIdType.MESH
F32 = jnp.float32
BF16 = jnp.bfloat16
NZ, NX, NY = 16, 4, 4
PLANE = NX * NY
LAG = 4
EARLY = 10


def kernel(
    scale,
    table_ref, points_ref, orbitals_ref, out_ref,
    orb_ref, hot, masked, parts, rows, grid, fields, stage, tiles, got,
    rs_send, rs_recv, grid_send, grid_recv, gridx_send, rows_send, rows_recv, rowsy_send,
    pair_send, pair_recv, tile_send, tile_recv, orb_sem,
):
    kdev, slab, channels = orb_ref.shape
    half = channels // 2
    chunk = slab // NZ
    total_k = kdev * 4 * NZ
    me, g = lax.axis_index("ka"), lax.axis_index("ga")
    z, x_hi, core = me // 4, (me // 2) % 2, me % 2
    y, x_lo = g // 2, g % 2
    x = 2 * x_hi + x_lo
    place = x * NY + y
    in_turn = (1 - (z // 8 - x_lo) ** 2) * (1 - (core - x_lo) ** 2)

    def in_plane(xx, yy):
        return {"ka": 4 * z + 2 * (xx // 2) + core, "ga": 2 * yy + xx % 2}

    def send(src, dst, send_sem, recv_sem, to):
        pltpu.make_async_remote_copy(
            src_ref=src, dst_ref=dst, send_sem=send_sem, recv_sem=recv_sem,
            device_id=to, device_id_type=MESH).start()

    def drain(ref, sem):
        pltpu.make_async_copy(ref, ref, sem).wait()

    fetch = pltpu.make_async_copy(orbitals_ref, orb_ref, orb_sem)
    fetch.start()
    barrier = pltpu.get_barrier_semaphore()

    def greet(to):
        pl.semaphore_signal(barrier, inc=1, device_id=to, device_id_type=MESH)

    @pl.loop(1, NZ)
    def _(i):
        greet({"ka": (me + 4 * i) % (4 * NZ)})

    @pl.loop(1, PLANE)
    def _(i):
        to = (place + i) % PLANE
        greet(in_plane(to // NY, to % NY))

    greet({"ka": me + 1 - 2 * core})

    @pl.loop(0, NZ)
    def _(zz):
        @pl.when((in_turn == 0) | (zz != z))
        def _():
            greet({"ka": 4 * zz + 2 * x_hi + x_lo, "ga": 2 * y + z // 8})

    index = jnp.broadcast_to(points_ref[...].astype(F32), (128, points_ref.shape[1])).T
    lane = lax.broadcasted_iota(jnp.int32, index.shape, 1) + g * slab
    for first in range(0, slab, 128):
        hot[:, first:first + 128] = (index == (lane + first).astype(F32)).astype(F32).astype(BF16)
    fetch.wait()
    for k in range(kdev):
        picked = jnp.dot(hot[...], orb_ref[k], preferred_element_type=F32)
        masked[k] = picked.astype(BF16).reshape(masked.shape[1:])

    pl.semaphore_wait(barrier, (NZ - 1) + (PLANE - 1) + 1 + NZ - in_turn)

    for k in range(kdev):
        @pl.loop(1, PLANE)
        def _(i):
            to = (place + i) % PLANE
            xx, yy = to // NY, to % NY
            send(masked.at[k, 4 * (xx % 2) + yy, :, xx // 2], parts.at[k, place],
                 rs_send, rs_recv.at[k], in_plane(xx, yy))

    def ship_grid(distance, k):
        for step in (distance, NZ - distance)[:2 if distance < NZ // 2 else 1]:
            zz = (z + step) % NZ
            send(orb_ref.at[k, pl.ds(pl.multiple_of(chunk * zz, chunk), chunk)], grid.at[x, z, k],
                 grid_send, grid_recv.at[x, z], {"ka": 4 * zz + me % 4})

    ships = [(distance, k) for distance in range(1, NZ // 2 + 1) for k in range(kdev)]
    for ship in ships[:EARLY]:
        ship_grid(*ship)

    def spread_grid(zz):
        @pl.loop(1, NX)
        def _(i):
            send(grid.at[x, zz], grid.at[x, zz], gridx_send, grid_recv.at[x, zz],
                 in_plane((x + i) % NX, y))

    def hand_rows(yy, zz, k, send_sem, to):
        send(rows.at[yy, zz, k], rows.at[yy, zz, k], send_sem, rows_recv.at[yy, zz, k], to)

    def wait_rows(yy, zz, k):
        drain(rows.at[yy, zz, k], rows_recv.at[yy, zz, k])

    def spread_rows(zz, k):
        for to in (1, NY - 1):
            hand_rows(y, zz, k, rowsy_send, in_plane(x, (y + to) % NY))

    def relay_rows(zz, k):
        source = (y + NY - 1 + 2 * (zz % 2)) % NY
        wait_rows(source, zz, k)
        hand_rows(source, zz, k, rowsy_send, in_plane(x, (y + 1 + 2 * (zz % 2)) % NY))

    def pass_rows(zz, k, to):
        hand_rows(y, zz, k, rows_send, {"ka": 4 * ((to + NZ) % NZ) + me % 4})

    def make_fields(zz):
        @pl.loop(1, NX)
        def _(j):
            xx = (x + j) % NX
            drain(grid.at[xx, zz], grid_recv.at[xx, zz])

        for yy in ((y + 1 + 2 * (zz % 2)) % NY, (y + 2) % NY):
            for k in range(kdev):
                wait_rows(yy, zz, k)
        for h in range(2):
            for k in range(kdev):
                picked = rows[:, zz, k, h].reshape(NY * 32, channels)
                stack = []
                for lo in (core, 1 - core):
                    phi = grid[2 * h + lo, zz, k]
                    stack += [phi, jnp.concatenate([phi[:, half:], -phi[:, :half]], axis=1)]
                field = lax.dot_general(
                    jnp.concatenate(stack, axis=0), picked, (((1,), (1,)), ((), ())),
                    preferred_element_type=F32).astype(BF16)
                fields[8 * zz + 4 * h + 2 * core + k] = field[:2 * chunk]
                stage[zz, h, k] = field[2 * chunk:]
            send(stage.at[zz, h], fields.at[pl.ds(8 * zz + 4 * h + 2 * core, kdev)],
                 pair_send, pair_recv, {"ka": me + 1 - 2 * core})

    grid[x, z] = orb_ref[:, pl.ds(pl.multiple_of(chunk * z, chunk), chunk), :]
    spread_grid(z)

    for k in range(kdev):
        parts[k, place] = masked[k, 4 * x_lo + y, :, x_hi]
        drain(parts.at[k, pl.ds(0, PLANE - 1)], rs_recv.at[k])
        for h in range(2):
            summed = parts[k, 8 * h].astype(F32)
            for i in range(1, 8):
                summed = summed + parts[k, 8 * h + i].astype(F32)
            rows[y, z, k, h] = summed.astype(BF16)
        pass_rows(z, k, z + 1)
        pass_rows(z, k, z - 1)
        spread_rows(z, k)
    for ship in ships[EARLY:EARLY + 1]:
        ship_grid(*ship)

    def both_ways(distance):
        return [(z + NZ - distance) % NZ, (z + distance) % NZ][:1 + (0 < distance < NZ // 2)]

    for t in range(1, NZ // 2 + 1):
        for k in range(kdev):
            for zz, ahead in zip(both_ways(t), (1, -1)):
                wait_rows(y, zz, k)
                if t < NZ // 2 - (ahead < 0):
                    pass_rows(zz, k, z + ahead)
                spread_rows(zz, k)
        for ship in ships[EARLY + t:EARLY + t + 1]:
            ship_grid(*ship)
        for zz in both_ways(t):
            drain(grid.at[x, zz], grid_recv.at[x, zz])
            spread_grid(zz)
        if t >= 2:
            for k in range(kdev):
                for zz in both_ways(t - 2):
                    relay_rows(zz, k)
        if t >= LAG:
            for zz in both_ways(t - LAG):
                make_fields(zz)
    for distance in (NZ // 2 - 1, NZ // 2):
        for k in range(kdev):
            for zz in both_ways(distance):
                relay_rows(zz, k)
    for distance in range(NZ // 2 + 1 - LAG, NZ // 2 + 1):
        for zz in both_ways(distance):
            make_fields(zz)

    drain(stage, pair_recv)

    shifts = [table_ref[q, 0] for q in range(2)]

    def step(k, totals):
        own = fields[k].astype(F32)
        own_re, own_im = own[:chunk], own[chunk:]
        new = []
        for q in range(2):
            other = fields[lax.rem(k + shifts[q], total_k)].astype(F32)
            re, im = other[:chunk], other[chunk:]
            new.append(totals[2 * q] + (own_re * re + own_im * im))
            new.append(totals[2 * q + 1] + (own_im * re - own_re * im))
        return tuple(new)

    zero = jnp.zeros((chunk, 128), F32)
    totals = lax.fori_loop(0, total_k, step, (zero,) * 4, unroll=4)
    tiles[...] = (jnp.concatenate(totals, axis=0) * scale).T.reshape(tiles.shape)

    @pl.loop(0, 16)
    def _(j):
        zz, cc = 8 * x_lo + j // 2, j % 2
        stays = (in_turn == 1) & (zz == z) & (cc == core)

        @pl.when(stays)
        def _():
            pltpu.make_async_copy(tiles.at[j], got.at[z], tile_recv).start()

        @pl.when(jnp.logical_not(stays))
        def _():
            send(tiles.at[j], got.at[z], tile_send, tile_recv,
                 {"ka": 4 * zz + 2 * x_hi + cc, "ga": 2 * y + core})

    drain(got, tile_recv)
    for i in range(4):
        out_ref[i] = jnp.concatenate(
            [got[zz, :, chunk * i:chunk * (i + 1)] for zz in range(NZ)], axis=1)

    drain(parts.at[:, pl.ds(0, PLANE - 1)], rs_send)
    drain(grid.at[0, pl.ds(0, NZ - 1)], grid_send)
    drain(grid.at[pl.ds(0, NX - 1)], gridx_send)
    drain(rows.at[0, pl.ds(0, NZ - 1)], rows_send)
    drain(rows.at[pl.ds(0, NY - 1)], rowsy_send)
    drain(stage, pair_send)

    @pl.when(in_turn == 1)
    def _():
        drain(tiles.at[pl.ds(0, 15)], tile_send)

    @pl.when(in_turn == 0)
    def _():
        drain(tiles, tile_send)


def on_device(orbitals, minus_table, points):
    kdev, slab, channels = orbitals.shape
    npts = points.shape[0]
    total_k = kdev * 4 * NZ
    chunk = slab // NZ
    vmem = pl.BlockSpec(memory_space=pltpu.VMEM)
    dma = pltpu.SemaphoreType.DMA
    out = pl.pallas_call(
        functools.partial(kernel, 1.0 / math.sqrt(total_k)),
        out_shape=jax.ShapeDtypeStruct((4, 8, slab), F32),
        in_specs=[pl.BlockSpec(memory_space=pltpu.SMEM), vmem, pl.BlockSpec(memory_space=pl.ANY)],
        out_specs=vmem,
        scratch_shapes=[
            pltpu.VMEM((kdev, slab, channels), BF16),
            pltpu.VMEM((npts, slab), BF16),
            pltpu.VMEM((kdev, 8, 2, 2, 16, channels), BF16),
            pltpu.VMEM((kdev, PLANE, 2, 16, channels), BF16),
            pltpu.VMEM((NY, NZ, kdev, 2, 2, 16, channels), BF16),
            pltpu.VMEM((NX, NZ, kdev, chunk, channels), BF16),
            pltpu.VMEM((total_k, 2 * chunk, 128), BF16),
            pltpu.VMEM((NZ, 2, kdev, 2 * chunk, 128), BF16),
            pltpu.VMEM((16, 8, 128), F32),
            pltpu.VMEM((NZ, 8, 128), F32),
            dma, dma((kdev,)), dma, dma((NX, NZ)), dma, dma, dma((NY, NZ, kdev)), dma,
            dma, dma, dma, dma, dma,
        ],
        compiler_params=pltpu.CompilerParams(
            collective_id=0, has_side_effects=True, vmem_limit_bytes=60 * 1024 * 1024),
    )(minus_table, points.reshape(1, npts), orbitals)
    return out.reshape(2, 2, 8, slab).transpose(2, 0, 1, 3)


def solution(mesh):
    placed = (P("ka", "ga", None), P(), P())
    return jax.shard_map(
        on_device, mesh=mesh, in_specs=placed, out_specs=P("ka", None, None, "ga"), check_vma=False
    )
```

```python
import functools
import math

import jax
import jax.numpy as jnp
from jax import lax
from jax.experimental import pallas as pl
from jax.experimental.pallas import tpu as pltpu
from jax.sharding import PartitionSpec as P

MESH = pl.DeviceIdType.MESH
F32 = jnp.float32
BF16 = jnp.bfloat16
NZ, NX, NY = 16, 4, 4
PLANE = NX * NY
LAG = 4
EARLY = 9


def kernel(
    scale,
    table_ref, points_ref, orbitals_ref, out_ref,
    orb_ref, hot, masked, parts, rows, grid, fields, stage, tiles, got,
    rs_send, rs_recv, grid_send, grid_recv, gridx_send, rows_send, rows_recv, rowsy_send,
    pair_send, pair_recv, tile_send, tile_recv, orb_sem,
):
    kdev, slab, channels = orb_ref.shape
    half = channels // 2
    chunk = slab // NZ
    total_k = kdev * 4 * NZ
    me, g = lax.axis_index("ka"), lax.axis_index("ga")
    z, x_hi, core = me // 4, (me // 2) % 2, me % 2
    y, x_lo = g // 2, g % 2
    x = 2 * x_hi + x_lo
    place = x * NY + y
    in_turn = (1 - (z // 8 - x_lo) ** 2) * (1 - (core - x_lo) ** 2)

    def in_plane(xx, yy):
        return {"ka": 4 * z + 2 * (xx // 2) + core, "ga": 2 * yy + xx % 2}

    def send(src, dst, send_sem, recv_sem, to):
        pltpu.make_async_remote_copy(
            src_ref=src, dst_ref=dst, send_sem=send_sem, recv_sem=recv_sem,
            device_id=to, device_id_type=MESH).start()

    def drain(ref, sem):
        pltpu.make_async_copy(ref, ref, sem).wait()

    fetch = pltpu.make_async_copy(orbitals_ref, orb_ref, orb_sem)
    fetch.start()
    barrier = pltpu.get_barrier_semaphore()

    def greet(to):
        pl.semaphore_signal(barrier, inc=1, device_id=to, device_id_type=MESH)

    def far_first(i):
        return (z + NZ // 2 + ((i + 1) // 2) * (2 * (i % 2) - 1) + NZ) % NZ

    @pl.loop(0, NZ)
    def _(i):
        zz = far_first(i)

        @pl.when((in_turn == 0) | (zz != z))
        def _():
            greet({"ka": 4 * zz + 2 * x_hi + x_lo, "ga": 2 * y + z // 8})

        @pl.when(zz != z)
        def _():
            greet({"ka": 4 * zz + me % 4})

    @pl.loop(1, PLANE)
    def _(i):
        to = (place + i) % PLANE
        greet(in_plane(to // NY, to % NY))

    greet({"ka": me + 1 - 2 * core})

    index = jnp.broadcast_to(points_ref[...].astype(F32), (128, points_ref.shape[1])).T
    lane = lax.broadcasted_iota(jnp.int32, index.shape, 1) + g * slab
    for first in range(0, slab, 128):
        hot[:, first:first + 128] = (index == (lane + first).astype(F32)).astype(F32).astype(BF16)
    fetch.wait()
    for k in range(kdev):
        picked = jnp.dot(hot[...], orb_ref[k], preferred_element_type=F32)
        masked[k] = picked.astype(BF16).reshape(masked.shape[1:])

    pl.semaphore_wait(barrier, (NZ - 1) + (PLANE - 1) + 1 + NZ - in_turn)

    for k in range(kdev):
        @pl.loop(1, PLANE)
        def _(i):
            to = (place + i) % PLANE
            xx, yy = to // NY, to % NY
            send(masked.at[k, 4 * (xx % 2) + yy, :, xx // 2], parts.at[k, place],
                 rs_send, rs_recv.at[k], in_plane(xx, yy))

    def ship_grid(distance, k):
        for step in (distance, NZ - distance)[:2 if distance < NZ // 2 else 1]:
            zz = (z + step) % NZ
            send(orb_ref.at[k, pl.ds(pl.multiple_of(chunk * zz, chunk), chunk)], grid.at[x, z, k],
                 grid_send, grid_recv.at[x, z], {"ka": 4 * zz + me % 4})

    ships = [(distance, k) for distance in range(1, NZ // 2 + 1) for k in range(kdev)]
    for ship in ships[:EARLY]:
        ship_grid(*ship)

    def spread_grid(zz):
        @pl.loop(1, NX)
        def _(i):
            send(grid.at[x, zz], grid.at[x, zz], gridx_send, grid_recv.at[x, zz],
                 in_plane((x + i) % NX, y))

    def hand_rows(yy, zz, k, send_sem, to):
        send(rows.at[yy, zz, k], rows.at[yy, zz, k], send_sem, rows_recv.at[yy, zz, k], to)

    def wait_rows(yy, zz, k):
        drain(rows.at[yy, zz, k], rows_recv.at[yy, zz, k])

    def spread_rows(zz, k):
        for to in (1, NY - 1):
            hand_rows(y, zz, k, rowsy_send, in_plane(x, (y + to) % NY))

    def relay_rows(zz, k):
        source = (y + NY - 1 + 2 * (k % 2)) % NY
        wait_rows(source, zz, k)
        hand_rows(source, zz, k, rowsy_send, in_plane(x, (y + 1 + 2 * (k % 2)) % NY))

    def pass_rows(zz, k, to):
        hand_rows(y, zz, k, rows_send, {"ka": 4 * ((to + NZ) % NZ) + me % 4})

    def make_fields(zz):
        @pl.loop(1, NX)
        def _(j):
            xx = (x + j) % NX
            drain(grid.at[xx, zz], grid_recv.at[xx, zz])

        for k in range(kdev):
            wait_rows((y + 1 + 2 * (k % 2)) % NY, zz, k)
            wait_rows((y + 2) % NY, zz, k)
        for h in range(2):
            for k in range(kdev):
                picked = rows[:, zz, k, h].reshape(NY * 32, channels)
                stack = []
                for lo in (core, 1 - core):
                    phi = grid[2 * h + lo, zz, k]
                    stack += [phi, jnp.concatenate([phi[:, half:], -phi[:, :half]], axis=1)]
                field = lax.dot_general(
                    jnp.concatenate(stack, axis=0), picked, (((1,), (1,)), ((), ())),
                    preferred_element_type=F32).astype(BF16)
                fields[8 * zz + 4 * h + 2 * core + k] = field[:2 * chunk]
                stage[zz, h, k] = field[2 * chunk:]
            send(stage.at[zz, h], fields.at[pl.ds(8 * zz + 4 * h + 2 * core, kdev)],
                 pair_send, pair_recv, {"ka": me + 1 - 2 * core})

    grid[x, z] = orb_ref[:, pl.ds(pl.multiple_of(chunk * z, chunk), chunk), :]
    spread_grid(z)

    for k in range(kdev):
        parts[k, place] = masked[k, 4 * x_lo + y, :, x_hi]
        drain(parts.at[k, pl.ds(0, PLANE - 1)], rs_recv.at[k])
        for h in range(2):
            summed = parts[k, 8 * h].astype(F32)
            for i in range(1, 8):
                summed = summed + parts[k, 8 * h + i].astype(F32)
            rows[y, z, k, h] = summed.astype(BF16)
        pass_rows(z, k, z + 1)
        pass_rows(z, k, z - 1)
        spread_rows(z, k)
    for ship in ships[EARLY:EARLY + 1]:
        ship_grid(*ship)

    def both_ways(distance):
        return [(z + NZ - distance) % NZ, (z + distance) % NZ][:1 + (0 < distance < NZ // 2)]

    for t in range(1, NZ // 2 + 1):
        for k in range(kdev):
            for zz, ahead in zip(both_ways(t), (1, -1)):
                wait_rows(y, zz, k)
                if t < NZ // 2 - (ahead < 0):
                    pass_rows(zz, k, z + ahead)
                spread_rows(zz, k)
        for ship in ships[EARLY + t:EARLY + t + 1]:
            ship_grid(*ship)
        for zz in both_ways(t):
            drain(grid.at[x, zz], grid_recv.at[x, zz])
            spread_grid(zz)
        for k in range(kdev):
            for zz in both_ways(t - 1):
                relay_rows(zz, k)
        if t >= LAG:
            for zz in both_ways(t - LAG):
                make_fields(zz)
    for t in range(NZ // 2 + 1, NZ // 2 + 1 + LAG):
        for k in range(kdev):
            for zz in both_ways(t - 1) if t < NZ // 2 + 2 else ():
                relay_rows(zz, k)
        for zz in both_ways(t - LAG):
            make_fields(zz)

    drain(stage, pair_recv)

    shifts = [table_ref[q, 0] for q in range(2)]

    def step(k, totals):
        own = fields[k].astype(F32)
        own_re, own_im = own[:chunk], own[chunk:]
        new = []
        for q in range(2):
            other = fields[lax.rem(k + shifts[q], total_k)].astype(F32)
            re, im = other[:chunk], other[chunk:]
            new.append(totals[2 * q] + (own_re * re + own_im * im))
            new.append(totals[2 * q + 1] + (own_im * re - own_re * im))
        return tuple(new)

    zero = jnp.zeros((chunk, 128), F32)
    totals = lax.fori_loop(0, total_k, step, (zero,) * 4, unroll=8)
    tiles[...] = (jnp.concatenate(totals, axis=0) * scale).T.reshape(tiles.shape)

    @pl.loop(0, 16)
    def _(j):
        zz, cc = 8 * x_lo + j // 2, j % 2
        stays = (in_turn == 1) & (zz == z) & (cc == core)

        @pl.when(stays)
        def _():
            pltpu.make_async_copy(tiles.at[j], got.at[z], tile_recv).start()

        @pl.when(jnp.logical_not(stays))
        def _():
            send(tiles.at[j], got.at[z], tile_send, tile_recv,
                 {"ka": 4 * zz + 2 * x_hi + cc, "ga": 2 * y + core})

    drain(got, tile_recv)
    for i in range(4):
        out_ref[i] = jnp.concatenate(
            [got[zz, :, chunk * i:chunk * (i + 1)] for zz in range(NZ)], axis=1)

    drain(parts.at[:, pl.ds(0, PLANE - 1)], rs_send)
    drain(grid.at[0, pl.ds(0, NZ - 1)], grid_send)
    drain(grid.at[pl.ds(0, NX - 1)], gridx_send)
    drain(rows.at[0, pl.ds(0, NZ - 1)], rows_send)
    drain(rows.at[pl.ds(0, NY - 1)], rowsy_send)
    drain(stage, pair_send)

    @pl.when(in_turn == 1)
    def _():
        drain(tiles.at[pl.ds(0, 15)], tile_send)

    @pl.when(in_turn == 0)
    def _():
        drain(tiles, tile_send)


def on_device(orbitals, minus_table, points):
    kdev, slab, channels = orbitals.shape
    npts = points.shape[0]
    total_k = kdev * 4 * NZ
    chunk = slab // NZ
    vmem = pl.BlockSpec(memory_space=pltpu.VMEM)
    dma = pltpu.SemaphoreType.DMA
    out = pl.pallas_call(
        functools.partial(kernel, 1.0 / math.sqrt(total_k)),
        out_shape=jax.ShapeDtypeStruct((4, 8, slab), F32),
        in_specs=[pl.BlockSpec(memory_space=pltpu.SMEM), vmem, pl.BlockSpec(memory_space=pl.ANY)],
        out_specs=vmem,
        scratch_shapes=[
            pltpu.VMEM((kdev, slab, channels), BF16),
            pltpu.VMEM((npts, slab), BF16),
            pltpu.VMEM((kdev, 8, 2, 2, 16, channels), BF16),
            pltpu.VMEM((kdev, PLANE, 2, 16, channels), BF16),
            pltpu.VMEM((NY, NZ, kdev, 2, 2, 16, channels), BF16),
            pltpu.VMEM((NX, NZ, kdev, chunk, channels), BF16),
            pltpu.VMEM((total_k, 2 * chunk, 128), BF16),
            pltpu.VMEM((NZ, 2, kdev, 2 * chunk, 128), BF16),
            pltpu.VMEM((16, 8, 128), F32),
            pltpu.VMEM((NZ, 8, 128), F32),
            dma, dma((kdev,)), dma, dma((NX, NZ)), dma, dma, dma((NY, NZ, kdev)), dma,
            dma, dma, dma, dma, dma,
        ],
        compiler_params=pltpu.CompilerParams(
            collective_id=0, has_side_effects=True, vmem_limit_bytes=60 * 1024 * 1024),
    )(minus_table, points.reshape(1, npts), orbitals)
    return out.reshape(2, 2, 8, slab).transpose(2, 0, 1, 3)


def solution(mesh):
    placed = (P("ka", "ga", None), P(), P())
    return jax.shard_map(
        on_device, mesh=mesh, in_specs=placed, out_specs=P("ka", None, None, "ga"), check_vma=False
    )
```

```python
import functools
import math

import jax
import jax.numpy as jnp
from jax import lax
from jax.experimental import pallas as pl
from jax.experimental.pallas import tpu as pltpu
from jax.sharding import PartitionSpec as P

MESH = pl.DeviceIdType.MESH
F32 = jnp.float32
BF16 = jnp.bfloat16
NZ, NX, NY = 16, 4, 4
PLANE = NX * NY
LAG = 4
EARLY = 9


def kernel(
    scale,
    table_ref, points_ref, orbitals_ref, out_ref,
    orb_ref, hot, masked, parts, rows, grid, fields, stage, tiles, got,
    rs_send, rs_recv, grid_send, grid_recv, gridx_send, rows_send, rows_recv, rowsy_send,
    pair_send, pair_recv, tile_send, tile_recv, orb_sem,
):
    kdev, slab, channels = orb_ref.shape
    half = channels // 2
    chunk = slab // NZ
    total_k = kdev * 4 * NZ
    me, g = lax.axis_index("ka"), lax.axis_index("ga")
    z, x_hi, core = me // 4, (me // 2) % 2, me % 2
    y, x_lo = g // 2, g % 2
    x = 2 * x_hi + x_lo
    place = x * NY + y
    in_turn = (1 - (z // 8 - x_lo) ** 2) * (1 - (core - x_lo) ** 2)

    def in_plane(xx, yy):
        return {"ka": 4 * z + 2 * (xx // 2) + core, "ga": 2 * yy + xx % 2}

    def send(src, dst, send_sem, recv_sem, to):
        pltpu.make_async_remote_copy(
            src_ref=src, dst_ref=dst, send_sem=send_sem, recv_sem=recv_sem,
            device_id=to, device_id_type=MESH).start()

    def drain(ref, sem):
        pltpu.make_async_copy(ref, ref, sem).wait()

    fetch = pltpu.make_async_copy(orbitals_ref, orb_ref, orb_sem)
    fetch.start()
    barrier = pltpu.get_barrier_semaphore()

    def greet(to):
        pl.semaphore_signal(barrier, inc=1, device_id=to, device_id_type=MESH)

    def far_first(i):
        return (z + NZ // 2 + ((i + 1) // 2) * (2 * (i % 2) - 1) + NZ) % NZ

    @pl.loop(0, NZ)
    def _(i):
        zz = far_first(i)

        @pl.when((in_turn == 0) | (zz != z))
        def _():
            greet({"ka": 4 * zz + 2 * x_hi + x_lo, "ga": 2 * y + z // 8})

        @pl.when(zz != z)
        def _():
            greet({"ka": 4 * zz + me % 4})

    @pl.loop(1, PLANE)
    def _(i):
        to = (place + i) % PLANE
        greet(in_plane(to // NY, to % NY))

    greet({"ka": me + 1 - 2 * core})

    index = jnp.broadcast_to(points_ref[...].astype(F32), (128, points_ref.shape[1])).T
    lane = lax.broadcasted_iota(jnp.int32, index.shape, 1) + g * slab
    for first in range(0, slab, 128):
        hot[:, first:first + 128] = (index == (lane + first).astype(F32)).astype(F32).astype(BF16)
    fetch.wait()
    for k in range(kdev):
        picked = jnp.dot(hot[...], orb_ref[k], preferred_element_type=F32)
        masked[k] = picked.astype(BF16).reshape(masked.shape[1:])

    pl.semaphore_wait(barrier, (NZ - 1) + (PLANE - 1) + 1 + NZ - in_turn)

    def ship_masked(k):
        @pl.loop(1, PLANE)
        def _(i):
            to = (place + i) % PLANE
            xx, yy = to // NY, to % NY
            send(masked.at[k, 4 * (xx % 2) + yy, :, xx // 2], parts.at[k, place],
                 rs_send.at[k], rs_recv.at[k], in_plane(xx, yy))

    ship_masked(0)

    def ship_grid(distance, k):
        for step in (distance, NZ - distance)[:2 if distance < NZ // 2 else 1]:
            zz = (z + step) % NZ
            send(orb_ref.at[k, pl.ds(pl.multiple_of(chunk * zz, chunk), chunk)], grid.at[x, z, k],
                 grid_send, grid_recv.at[x, z], {"ka": 4 * zz + me % 4})

    ships = [(distance, k) for distance in range(1, NZ // 2 + 1) for k in range(kdev)]
    for ship in ships[:EARLY]:
        ship_grid(*ship)

    ship_masked(1)

    def spread_grid(zz):
        @pl.loop(1, NX)
        def _(i):
            send(grid.at[x, zz], grid.at[x, zz], gridx_send, grid_recv.at[x, zz],
                 in_plane((x + i) % NX, y))

    def hand_rows(yy, zz, k, send_sem, to):
        send(rows.at[yy, zz, k], rows.at[yy, zz, k], send_sem, rows_recv.at[yy, zz, k], to)

    def wait_rows(yy, zz, k):
        drain(rows.at[yy, zz, k], rows_recv.at[yy, zz, k])

    def spread_rows(zz, k):
        for to in (1, NY - 1):
            hand_rows(y, zz, k, rowsy_send, in_plane(x, (y + to) % NY))

    def relay_rows(zz, k):
        source = (y + NY - 1 + 2 * (k % 2)) % NY
        wait_rows(source, zz, k)
        hand_rows(source, zz, k, rowsy_send, in_plane(x, (y + 1 + 2 * (k % 2)) % NY))

    def pass_rows(zz, k, to):
        hand_rows(y, zz, k, rows_send, {"ka": 4 * ((to + NZ) % NZ) + me % 4})

    def make_fields(zz):
        @pl.loop(1, NX)
        def _(j):
            xx = (x + j) % NX
            drain(grid.at[xx, zz], grid_recv.at[xx, zz])

        for k in range(kdev):
            wait_rows((y + 1 + 2 * (k % 2)) % NY, zz, k)
            wait_rows((y + 2) % NY, zz, k)
        for h in range(2):
            for k in range(kdev):
                picked = rows[:, zz, k, h].reshape(NY * 32, channels)
                stack = []
                for lo in (core, 1 - core):
                    phi = grid[2 * h + lo, zz, k]
                    stack += [phi, jnp.concatenate([phi[:, half:], -phi[:, :half]], axis=1)]
                field = lax.dot_general(
                    jnp.concatenate(stack, axis=0), picked, (((1,), (1,)), ((), ())),
                    preferred_element_type=F32).astype(BF16)
                fields[8 * zz + 4 * h + 2 * core + k] = field[:2 * chunk]
                stage[zz, h, k] = field[2 * chunk:]
            send(stage.at[zz, h], fields.at[pl.ds(8 * zz + 4 * h + 2 * core, kdev)],
                 pair_send, pair_recv, {"ka": me + 1 - 2 * core})

    grid[x, z] = orb_ref[:, pl.ds(pl.multiple_of(chunk * z, chunk), chunk), :]
    spread_grid(z)

    for k in range(kdev):
        parts[k, place] = masked[k, 4 * x_lo + y, :, x_hi]
        drain(parts.at[k, pl.ds(0, PLANE - 1)], rs_recv.at[k])
        for h in range(2):
            summed = parts[k, 8 * h].astype(F32)
            for i in range(1, 8):
                summed = summed + parts[k, 8 * h + i].astype(F32)
            rows[y, z, k, h] = summed.astype(BF16)
        pass_rows(z, k, z + 1)
        pass_rows(z, k, z - 1)
        spread_rows(z, k)
    for ship in ships[EARLY:EARLY + 1]:
        ship_grid(*ship)

    def both_ways(distance):
        return [(z + NZ - distance) % NZ, (z + distance) % NZ][:1 + (0 < distance < NZ // 2)]

    for t in range(1, NZ // 2 + 1):
        for k in range(kdev):
            for zz, ahead in zip(both_ways(t), (1, -1)):
                wait_rows(y, zz, k)
                if t < NZ // 2 - (ahead < 0):
                    pass_rows(zz, k, z + ahead)
                spread_rows(zz, k)
        for ship in ships[EARLY + t:EARLY + t + 1]:
            ship_grid(*ship)
        for zz in both_ways(t):
            drain(grid.at[x, zz], grid_recv.at[x, zz])
            spread_grid(zz)
        for k in range(kdev):
            for zz in both_ways(t - 1):
                relay_rows(zz, k)
        if t >= LAG:
            for zz in both_ways(t - LAG):
                make_fields(zz)
    for t in range(NZ // 2 + 1, NZ // 2 + 1 + LAG):
        for k in range(kdev):
            for zz in both_ways(t - 1) if t < NZ // 2 + 2 else ():
                relay_rows(zz, k)
        for zz in both_ways(t - LAG):
            make_fields(zz)

    drain(stage, pair_recv)

    shifts = [table_ref[q, 0] for q in range(2)]

    def step(k, totals):
        own = fields[k].astype(F32)
        own_re, own_im = own[:chunk], own[chunk:]
        new = []
        for q in range(2):
            other = fields[lax.rem(k + shifts[q], total_k)].astype(F32)
            re, im = other[:chunk], other[chunk:]
            new.append(totals[2 * q] + (own_re * re + own_im * im))
            new.append(totals[2 * q + 1] + (own_im * re - own_re * im))
        return tuple(new)

    zero = jnp.zeros((chunk, 128), F32)
    totals = lax.fori_loop(0, total_k, step, (zero,) * 4, unroll=8)
    tiles[...] = (jnp.concatenate(totals, axis=0) * scale).T.reshape(tiles.shape)

    @pl.loop(0, 16)
    def _(j):
        zz, cc = 8 * x_lo + j // 2, j % 2
        stays = (in_turn == 1) & (zz == z) & (cc == core)

        @pl.when(stays)
        def _():
            pltpu.make_async_copy(tiles.at[j], got.at[z], tile_recv).start()

        @pl.when(jnp.logical_not(stays))
        def _():
            send(tiles.at[j], got.at[z], tile_send, tile_recv,
                 {"ka": 4 * zz + 2 * x_hi + cc, "ga": 2 * y + core})

    drain(got, tile_recv)
    for i in range(4):
        out_ref[i] = jnp.concatenate(
            [got[zz, :, chunk * i:chunk * (i + 1)] for zz in range(NZ)], axis=1)

    for k in range(kdev):
        drain(parts.at[k, pl.ds(0, PLANE - 1)], rs_send.at[k])
    drain(grid.at[0, pl.ds(0, NZ - 1)], grid_send)
    drain(grid.at[pl.ds(0, NX - 1)], gridx_send)
    drain(rows.at[0, pl.ds(0, NZ - 1)], rows_send)
    drain(rows.at[pl.ds(0, NY - 1)], rowsy_send)
    drain(stage, pair_send)

    @pl.when(in_turn == 1)
    def _():
        drain(tiles.at[pl.ds(0, 15)], tile_send)

    @pl.when(in_turn == 0)
    def _():
        drain(tiles, tile_send)


def on_device(orbitals, minus_table, points):
    kdev, slab, channels = orbitals.shape
    npts = points.shape[0]
    total_k = kdev * 4 * NZ
    chunk = slab // NZ
    vmem = pl.BlockSpec(memory_space=pltpu.VMEM)
    dma = pltpu.SemaphoreType.DMA
    out = pl.pallas_call(
        functools.partial(kernel, 1.0 / math.sqrt(total_k)),
        out_shape=jax.ShapeDtypeStruct((4, 8, slab), F32),
        in_specs=[pl.BlockSpec(memory_space=pltpu.SMEM), vmem, pl.BlockSpec(memory_space=pl.ANY)],
        out_specs=vmem,
        scratch_shapes=[
            pltpu.VMEM((kdev, slab, channels), BF16),
            pltpu.VMEM((npts, slab), BF16),
            pltpu.VMEM((kdev, 8, 2, 2, 16, channels), BF16),
            pltpu.VMEM((kdev, PLANE, 2, 16, channels), BF16),
            pltpu.VMEM((NY, NZ, kdev, 2, 2, 16, channels), BF16),
            pltpu.VMEM((NX, NZ, kdev, chunk, channels), BF16),
            pltpu.VMEM((total_k, 2 * chunk, 128), BF16),
            pltpu.VMEM((NZ, 2, kdev, 2 * chunk, 128), BF16),
            pltpu.VMEM((16, 8, 128), F32),
            pltpu.VMEM((NZ, 8, 128), F32),
            dma((kdev,)), dma((kdev,)), dma, dma((NX, NZ)), dma, dma, dma((NY, NZ, kdev)), dma,
            dma, dma, dma, dma, dma,
        ],
        compiler_params=pltpu.CompilerParams(
            collective_id=0, has_side_effects=True, vmem_limit_bytes=60 * 1024 * 1024),
    )(minus_table, points.reshape(1, npts), orbitals)
    return out.reshape(2, 2, 8, slab).transpose(2, 0, 1, 3)


def solution(mesh):
    placed = (P("ka", "ga", None), P(), P())
    return jax.shard_map(
        on_device, mesh=mesh, in_specs=placed, out_specs=P("ka", None, None, "ga"), check_vma=False
    )
```

```python
import functools
import math

import jax
import jax.numpy as jnp
from jax import lax
from jax.experimental import pallas as pl
from jax.experimental.pallas import tpu as pltpu
from jax.sharding import PartitionSpec as P

MESH = pl.DeviceIdType.MESH
F32 = jnp.float32
BF16 = jnp.bfloat16
NZ, NX, NY = 16, 4, 4
PLANE = NX * NY
LAG = 4
EARLY = 9


def kernel(
    scale,
    table_ref, points_ref, orbitals_ref, out_ref,
    orb_ref, hot, masked, parts, rows, grid, fields, stage, tiles, got,
    rs_send, rs_recv, grid_send, grid_recv, gridx_send, rows_send, rows_recv, rowsy_send,
    pair_send, pair_recv, tile_send, tile_recv, orb_sem,
):
    kdev, slab, channels = orb_ref.shape
    half = channels // 2
    chunk = slab // NZ
    total_k = kdev * 4 * NZ
    me, g = lax.axis_index("ka"), lax.axis_index("ga")
    z, x_hi, core = me // 4, (me // 2) % 2, me % 2
    y, x_lo = g // 2, g % 2
    x = 2 * x_hi + x_lo
    place = x * NY + y
    in_turn = (1 - (z // 8 - x_lo) ** 2) * (1 - (core - x_lo) ** 2)

    def in_plane(xx, yy):
        return {"ka": 4 * z + 2 * (xx // 2) + core, "ga": 2 * yy + xx % 2}

    def send(src, dst, send_sem, recv_sem, to):
        pltpu.make_async_remote_copy(
            src_ref=src, dst_ref=dst, send_sem=send_sem, recv_sem=recv_sem,
            device_id=to, device_id_type=MESH).start()

    def drain(ref, sem):
        pltpu.make_async_copy(ref, ref, sem).wait()

    fetch = pltpu.make_async_copy(orbitals_ref, orb_ref, orb_sem)
    fetch.start()
    barrier = pltpu.get_barrier_semaphore()

    def greet(to):
        pl.semaphore_signal(barrier, inc=1, device_id=to, device_id_type=MESH)

    def far_first(i):
        return (z + NZ // 2 + ((i + 1) // 2) * (2 * (i % 2) - 1) + NZ) % NZ

    @pl.loop(0, NZ)
    def _(i):
        zz = far_first(i)

        @pl.when((in_turn == 0) | (zz != z))
        def _():
            greet({"ka": 4 * zz + 2 * x_hi + x_lo, "ga": 2 * y + z // 8})

        @pl.when(zz != z)
        def _():
            greet({"ka": 4 * zz + me % 4})

    @pl.loop(1, PLANE)
    def _(i):
        to = (place + i) % PLANE
        greet(in_plane(to // NY, to % NY))

    greet({"ka": me + 1 - 2 * core})

    index = jnp.broadcast_to(points_ref[...].astype(F32), (128, points_ref.shape[1])).T
    lane = lax.broadcasted_iota(jnp.int32, index.shape, 1) + g * slab
    for first in range(0, slab, 128):
        hot[:, first:first + 128] = (index == (lane + first).astype(F32)).astype(F32).astype(BF16)
    fetch.wait()
    for k in range(kdev):
        picked = jnp.dot(hot[...], orb_ref[k], preferred_element_type=F32)
        masked[k] = picked.astype(BF16).reshape(masked.shape[1:])

    pl.semaphore_wait(barrier, (NZ - 1) + (PLANE - 1) + 1 + NZ - in_turn)

    def ship_masked(k):
        @pl.loop(1, PLANE)
        def _(i):
            to = (place + i) % PLANE
            xx, yy = to // NY, to % NY
            send(masked.at[k, 4 * (xx % 2) + yy, :, xx // 2], parts.at[k, place],
                 rs_send.at[k], rs_recv.at[k], in_plane(xx, yy))

    ship_masked(0)

    def ship_grid(distance, k):
        for step in (distance, NZ - distance)[:2 if distance < NZ // 2 else 1]:
            zz = (z + step) % NZ
            send(orb_ref.at[k, pl.ds(pl.multiple_of(chunk * zz, chunk), chunk)], grid.at[x, z, k],
                 grid_send, grid_recv.at[x, z], {"ka": 4 * zz + me % 4})

    ships = [(distance, k) for distance in range(1, NZ // 2 + 1) for k in range(kdev)]
    for ship in ships[:EARLY]:
        ship_grid(*ship)

    ship_masked(1)

    def spread_grid(zz):
        @pl.loop(1, NX)
        def _(i):
            send(grid.at[x, zz], grid.at[x, zz], gridx_send, grid_recv.at[x, zz],
                 in_plane((x + i) % NX, y))

    def hand_rows(yy, zz, k, send_sem, to):
        send(rows.at[yy, zz, k], rows.at[yy, zz, k], send_sem, rows_recv.at[yy, zz, k], to)

    def wait_rows(yy, zz, k):
        drain(rows.at[yy, zz, k], rows_recv.at[yy, zz, k])

    def spread_rows(zz, k):
        for to in (1, NY - 1):
            hand_rows(y, zz, k, rowsy_send, in_plane(x, (y + to) % NY))

    def relay_rows(zz, k):
        source = (y + NY - 1 + 2 * (k % 2)) % NY
        wait_rows(source, zz, k)
        hand_rows(source, zz, k, rowsy_send, in_plane(x, (y + 1 + 2 * (k % 2)) % NY))

    def pass_rows(zz, k, to):
        hand_rows(y, zz, k, rows_send, {"ka": 4 * ((to + NZ) % NZ) + me % 4})

    def make_fields(zz):
        @pl.loop(1, NX)
        def _(j):
            xx = (x + j) % NX
            drain(grid.at[xx, zz], grid_recv.at[xx, zz])

        for k in range(kdev):
            wait_rows((y + 1 + 2 * (k % 2)) % NY, zz, k)
            wait_rows((y + 2) % NY, zz, k)
        for h in range(2):
            for k in range(kdev):
                picked = rows[:, zz, k, h].reshape(NY * 32, channels)
                stack = []
                for lo in (core, 1 - core):
                    phi = grid[2 * h + lo, zz, k]
                    stack += [phi, jnp.concatenate([phi[:, half:], -phi[:, :half]], axis=1)]
                field = lax.dot_general(
                    jnp.concatenate(stack, axis=0), picked, (((1,), (1,)), ((), ())),
                    preferred_element_type=F32).astype(BF16)
                fields[8 * zz + 4 * h + 2 * core + k] = field[:2 * chunk]
                stage[zz, h, k] = field[2 * chunk:]
            send(stage.at[zz, h], fields.at[pl.ds(8 * zz + 4 * h + 2 * core, kdev)],
                 pair_send, pair_recv, {"ka": me + 1 - 2 * core})

    grid[x, z] = orb_ref[:, pl.ds(pl.multiple_of(chunk * z, chunk), chunk), :]
    spread_grid(z)

    for k in range(kdev):
        parts[k, place] = masked[k, 4 * x_lo + y, :, x_hi]
        drain(parts.at[k, pl.ds(0, PLANE - 1)], rs_recv.at[k])
        for h in range(2):
            summed = parts[k, 8 * h].astype(F32)
            for i in range(1, 8):
                summed = summed + parts[k, 8 * h + i].astype(F32)
            rows[y, z, k, h] = summed.astype(BF16)
        pass_rows(z, k, z + 1)
        pass_rows(z, k, z - 1)
        spread_rows(z, k)
    for ship in ships[EARLY:EARLY + 1]:
        ship_grid(*ship)

    def both_ways(distance):
        return [(z + NZ - distance) % NZ, (z + distance) % NZ][:1 + (0 < distance < NZ // 2)]

    for t in range(1, NZ // 2 + 1):
        for k in range(kdev):
            for zz, ahead in zip(both_ways(t), (1, -1)):
                wait_rows(y, zz, k)
                if t < NZ // 2 - (ahead < 0):
                    pass_rows(zz, k, z + ahead)
                spread_rows(zz, k)
            if k == 0:
                for ship in ships[EARLY + t:EARLY + t + 1]:
                    ship_grid(*ship)
        for zz in both_ways(t):
            drain(grid.at[x, zz], grid_recv.at[x, zz])
            spread_grid(zz)
        for k in range(kdev):
            for zz in both_ways(t - 1):
                relay_rows(zz, k)
        if t >= LAG:
            for zz in both_ways(t - LAG):
                make_fields(zz)
    for t in range(NZ // 2 + 1, NZ // 2 + 1 + LAG):
        for k in range(kdev):
            for zz in both_ways(t - 1) if t < NZ // 2 + 2 else ():
                relay_rows(zz, k)
        for zz in both_ways(t - LAG):
            make_fields(zz)

    drain(stage, pair_recv)

    shifts = [table_ref[q, 0] for q in range(2)]

    def step(k, totals):
        own = fields[k].astype(F32)
        own_re, own_im = own[:chunk], own[chunk:]
        new = []
        for q in range(2):
            other = fields[lax.rem(k + shifts[q], total_k)].astype(F32)
            re, im = other[:chunk], other[chunk:]
            new.append(totals[2 * q] + (own_re * re + own_im * im))
            new.append(totals[2 * q + 1] + (own_im * re - own_re * im))
        return tuple(new)

    zero = jnp.zeros((chunk, 128), F32)
    totals = lax.fori_loop(0, total_k, step, (zero,) * 4, unroll=8)
    tiles[...] = (jnp.concatenate(totals, axis=0) * scale).T.reshape(tiles.shape)

    @pl.loop(0, 16)
    def _(j):
        zz, cc = 8 * x_lo + j // 2, j % 2
        stays = (in_turn == 1) & (zz == z) & (cc == core)

        @pl.when(stays)
        def _():
            pltpu.make_async_copy(tiles.at[j], got.at[z], tile_recv).start()

        @pl.when(jnp.logical_not(stays))
        def _():
            send(tiles.at[j], got.at[z], tile_send, tile_recv,
                 {"ka": 4 * zz + 2 * x_hi + cc, "ga": 2 * y + core})

    drain(got, tile_recv)
    for i in range(4):
        out_ref[i] = jnp.concatenate(
            [got[zz, :, chunk * i:chunk * (i + 1)] for zz in range(NZ)], axis=1)

    for k in range(kdev):
        drain(parts.at[k, pl.ds(0, PLANE - 1)], rs_send.at[k])
    drain(grid.at[0, pl.ds(0, NZ - 1)], grid_send)
    drain(grid.at[pl.ds(0, NX - 1)], gridx_send)
    drain(rows.at[0, pl.ds(0, NZ - 1)], rows_send)
    drain(rows.at[pl.ds(0, NY - 1)], rowsy_send)
    drain(stage, pair_send)

    @pl.when(in_turn == 1)
    def _():
        drain(tiles.at[pl.ds(0, 15)], tile_send)

    @pl.when(in_turn == 0)
    def _():
        drain(tiles, tile_send)


def on_device(orbitals, minus_table, points):
    kdev, slab, channels = orbitals.shape
    npts = points.shape[0]
    total_k = kdev * 4 * NZ
    chunk = slab // NZ
    vmem = pl.BlockSpec(memory_space=pltpu.VMEM)
    dma = pltpu.SemaphoreType.DMA
    out = pl.pallas_call(
        functools.partial(kernel, 1.0 / math.sqrt(total_k)),
        out_shape=jax.ShapeDtypeStruct((4, 8, slab), F32),
        in_specs=[pl.BlockSpec(memory_space=pltpu.SMEM), vmem, pl.BlockSpec(memory_space=pl.ANY)],
        out_specs=vmem,
        scratch_shapes=[
            pltpu.VMEM((kdev, slab, channels), BF16),
            pltpu.VMEM((npts, slab), BF16),
            pltpu.VMEM((kdev, 8, 2, 2, 16, channels), BF16),
            pltpu.VMEM((kdev, PLANE, 2, 16, channels), BF16),
            pltpu.VMEM((NY, NZ, kdev, 2, 2, 16, channels), BF16),
            pltpu.VMEM((NX, NZ, kdev, chunk, channels), BF16),
            pltpu.VMEM((total_k, 2 * chunk, 128), BF16),
            pltpu.VMEM((NZ, 2, kdev, 2 * chunk, 128), BF16),
            pltpu.VMEM((16, 8, 128), F32),
            pltpu.VMEM((NZ, 8, 128), F32),
            dma((kdev,)), dma((kdev,)), dma, dma((NX, NZ)), dma, dma, dma((NY, NZ, kdev)), dma,
            dma, dma, dma, dma, dma,
        ],
        compiler_params=pltpu.CompilerParams(
            collective_id=0, has_side_effects=True, vmem_limit_bytes=60 * 1024 * 1024),
    )(minus_table, points.reshape(1, npts), orbitals)
    return out.reshape(2, 2, 8, slab).transpose(2, 0, 1, 3)


def solution(mesh):
    placed = (P("ka", "ga", None), P(), P())
    return jax.shard_map(
        on_device, mesh=mesh, in_specs=placed, out_specs=P("ka", None, None, "ga"), check_vma=False
    )
```
